32 devices in a mesh: groups: 2 (over x), expert: 8 (over z, y), tensor: 2 (over core).
Axes of the slice: x: 2, y: 2, z: 4, core: 2. Of those that a mesh axis runs over, the one named last changes fastest.
Arguments:
- tokens: bfloat16 [2048, 4096], P(('groups', 'expert', 'tensor')), parts along dimension 0, may hold values from -6 to 6
- expert_ids: int32 [2048, 8], P(('groups', 'expert', 'tensor')), parts along dimension 0, may hold values from 0 to 31, all different within a row; in each aligned block of 64 rows (0 to 63, 64 to 127, ...) at most 20 rows name the same one
- route_weights: float32 [2048, 8], P(('groups', 'expert', 'tensor')), parts along dimension 0, may hold values from 0.1 to 1
- gate_weight: bfloat16 [32, 768, 4096], P('expert', 'tensor'), may hold values from -0.09375 to 0.09375
- up_weight: bfloat16 [32, 768, 4096], P('expert', 'tensor'), may hold values from -0.09375 to 0.09375
- down_weight: bfloat16 [32, 768, 4096], P('expert', 'tensor'), may hold values from -0.21875 to 0.21875
Outputs:
- combined: bfloat16 [2048, 4096], P(('groups', 'expert', 'tensor')), parts along dimension 0
The draws below stay inside these ranges and needn't reach their ends.
There are 2 independent parts, one for each index of `groups`. The reference program is written for one: setup_inputs(seed, part) draws one part's arguments, and reference() takes and returns one part's arrays. A program takes and returns all parts, laid end to end along the dimension named above; an argument that names none is the same for every part. Nothing has to cross between parts.
Inputs may be any that keep to these rules, and one draw needn't show every extreme that they name: `expert_ids`: each token names 8 different experts. Within each aligned block of 64 tokens no expert is named by more than 20 tokens, a bound that some block reaches.
All inputs are finite; a program needn't handle non-finite values.
Results may differ from the reference program's by a relative error of at most 0.008.
Values may be sent and summed in bfloat16 or wider, within the bound.
A program may use at most 192 MiB of HBM per device.

```python
import math
import jax
import jax.numpy as jnp
import numpy as np
from jax import lax

D = 4096
FF = 768
EXPERTS = 32
TOPK = 8
TOK_DEV = 64
CAP = 20
TOKENS = 1024


def block_levels(stream_key, extent, split, least, top_value):
    gain, own = 1.0, jax.random.fold_in(stream_key, 6)
    for position, blocks in split:
        draws = jnp.exp(jax.random.uniform(jax.random.fold_in(own, position), (blocks,), jnp.float32, least / len(split), top_value / len(split)))
        gain = gain * jnp.repeat(draws, extent[position] // blocks).reshape([-1 if axis == position else 1 for axis in range(len(extent))])
    return gain


def assign_block(key, own, number, rows, count, top, reach, skew):
    ranking = jax.random.permutation(key, count)
    crowded, usual = portions_of(count, rows * top, reach, skew, True), portions_of(count, rows * top, reach, skew, False)
    places = jnp.arange(count)

    def named(sizes, rotation):
        used = int((sizes > 0).sum())
        fixed = max(1, used // 4)
        moved = fixed + (places - fixed + rotation * (used - fixed)) % max(1, count - fixed)
        return jnp.zeros((count,), jnp.int32).at[ranking[jnp.where(places < fixed, places, moved)]].set(jnp.asarray(sizes, jnp.int32))

    sizes = jnp.where(number % 4 == 0, named(crowded, number // 4), named(usual, number - number // 4 - 1))
    mixed = jax.random.permutation(jax.random.fold_in(own, 3), count)
    source_of, taker = mixed[0:count // 2 * 2:2], mixed[1:count // 2 * 2:2]
    room = jnp.minimum(sizes[source_of] - 1, reach - sizes[taker]) // 2
    room = jnp.where((source_of == ranking[0]) | (taker == ranking[0]) | (sizes[taker] == 0), 0, jnp.maximum(room, 0))
    moved = jax.random.randint(jax.random.fold_in(own, 4), (count // 2,), 0, 1 << 20) % (room + 1)
    sizes = sizes.at[source_of].add(-moved).at[taker].add(moved)
    members = jnp.searchsorted(jnp.cumsum(sizes), jnp.arange(rows * top), side="right").astype(jnp.int32)
    listing = members.reshape(top, rows).T
    listing = listing[jax.random.permutation(jax.random.fold_in(own, 1), rows)]
    rotation = jax.random.randint(jax.random.fold_in(own, 2), (rows, 1), 0, top)
    return jnp.take_along_axis(listing, (jnp.arange(top)[None, :] + rotation) % top, axis=1)


def portions_of(number_of, total, reach, lean, full):
    portions = [(1 << 20) // math.isqrt(grade ** lean) + 1 for grade in range(1, number_of + 1)]
    largest = reach if full else min(reach, max(-(-total // number_of), total * portions[0] // sum(portions)))
    least = 1 if total - largest >= number_of - 1 else 0
    given, rest = [largest] + [least] * (number_of - 1), total - largest - least * (number_of - 1)
    while rest > 0:
        candidates = [i for i in range(1, number_of) if given[i] < largest] or [i for i in range(1, number_of) if given[i] < reach]
        whole, left = sum([portions[i] for i in candidates]), rest
        for i in candidates:
            more = min(reach - given[i], max(1, left * portions[i] // whole), rest)
            given[i] = given[i] + more
            rest = rest - more
    return np.array(given)


def bell_draw(own_key, dims, width, reach, pieces=(), kind=jnp.bfloat16):
    drawn = jax.random.normal(own_key, dims, jnp.float32) * width
    if len(pieces) > 0:
        drawn = block_levels(own_key, dims, pieces, -0.22, 0.18) * drawn
    return jnp.clip(drawn, min=-reach, max=reach).astype(kind)


def setup_inputs(seed: int = 0, part: int = 0) -> dict:
    streams_of = jax.random.split(jax.random.key(seed), 7)
    part_splits = jax.random.split(jax.random.fold_in(streams_of[6], part), 7)
    tokens = bell_draw(part_splits[0], (TOKENS, D), 1.0, 6.0, ((0, 16),))
    expert_ids_keys = jax.random.split(jax.random.fold_in(part_splits[1], 1), TOKENS // TOK_DEV)
    expert_ids_turns = jax.random.permutation(jax.random.fold_in(part_splits[1], 3), TOKENS // TOK_DEV)
    expert_ids = jax.vmap(lambda own, number: assign_block(jax.random.fold_in(part_splits[1], 2), own, number, TOK_DEV, EXPERTS, TOPK, CAP, 2))(expert_ids_keys, expert_ids_turns).reshape((TOKENS, TOPK))
    route_weights = jnp.clip(jnp.exp(math.log(1.0) - 2.3025851 * jax.random.uniform(part_splits[2], (TOKENS, TOPK), jnp.float32) ** block_levels(part_splits[2], (TOKENS, TOPK), ((0, 16),), -0.2, 0.2)), 0.1, 1.0)
    gate_weight = bell_draw(streams_of[3], (EXPERTS, FF, D), D ** -0.5, 0.09375, ((0, 8), (1, 2)))
    up_weight = bell_draw(streams_of[4], (EXPERTS, FF, D), D ** -0.5, 0.09375, ((0, 8), (1, 2)))
    down_weight = bell_draw(streams_of[5], (EXPERTS, FF, D), FF ** -0.5, 0.21875, ((0, 8), (1, 2)))
    return dict(tokens=tokens, expert_ids=expert_ids, route_weights=route_weights, gate_weight=gate_weight, up_weight=up_weight, down_weight=down_weight)


def slot_ranks(block_ids):
    labels = jnp.arange(EXPERTS, dtype=jnp.int32)
    chosen = jnp.sum((block_ids[:, :, None] == labels[None, None, :]).astype(jnp.int32), axis=1)
    before = jnp.cumsum(chosen, axis=0) - chosen
    return jnp.take_along_axis(before, block_ids, axis=1).astype(jnp.int32)


def expert_apply(row_block, gate_part, up_part, down_part):
    gate_value = lax.dot_general(row_block, gate_part, (((1,), (1,)), ((), ())), preferred_element_type=jnp.float32)
    up_value = lax.dot_general(row_block, up_part, (((1,), (1,)), ((), ())), preferred_element_type=jnp.float32)
    hidden = (jax.nn.silu(gate_value) * up_value).astype(jnp.bfloat16)
    return jnp.dot(hidden, down_part, preferred_element_type=jnp.float32).astype(jnp.bfloat16)


def reference(tokens, expert_ids, route_weights, gate_weight, up_weight, down_weight):
    blocks = TOKENS // TOK_DEV
    block_ids = expert_ids.reshape(blocks, TOK_DEV, TOPK).astype(jnp.int32)
    slot_rank = jax.vmap(slot_ranks)(block_ids)
    block_index = jnp.broadcast_to(jnp.arange(blocks, dtype=jnp.int32)[:, None, None], block_ids.shape)
    token_blocks = tokens.reshape(blocks, TOK_DEV, D)
    packed = jnp.zeros((EXPERTS, blocks, CAP, D), tokens.dtype)
    packed = packed.at[block_ids, block_index, slot_rank].set(token_blocks[:, :, None, :])

    def one_expert(item):
        rows, gate_part, up_part, down_part = item
        return expert_apply(rows.reshape(blocks * CAP, D), gate_part, up_part, down_part)

    expert_out = lax.map(one_expert, (packed, gate_weight, up_weight, down_weight))
    expert_out = expert_out.reshape(EXPERTS, blocks, CAP, D)
    picked = expert_out[block_ids, block_index, slot_rank]
    weights = route_weights.reshape(blocks, TOK_DEV, TOPK).astype(jnp.float32)
    combined = jnp.einsum("btk,btkd->btd", weights, picked.astype(jnp.float32))
    return combined.reshape(TOKENS, D).astype(jnp.bfloat16)
```

```python
import functools

import jax
import jax.numpy as jnp
from jax import lax
from jax.experimental import pallas as pl
from jax.experimental.pallas import tpu as pltpu
from jax.sharding import PartitionSpec as P

MESH = pl.DeviceIdType.MESH
EXTRA = 128
HID_TILE = 256
OUT_TILE = 512


def nearest(z, step):
    lower = 1 - z // 2
    edge = z * lower + (3 - z) * (1 - lower)
    near = step + edge * (1 - step // 2) * (1 - 2 * (step % 2))
    return near * lower + (3 - near) * (1 - lower)


def kernel(
    line, held, tokens_ref, ids_ref, route_ref, gate_ref, up_ref, down_ref, out_ref,
    tok, gate, up, down, hid, part, from_core, from_y, from_z,
    weight_sem, own_sem, zs, zr, ys, yr, cs, cr, pcs, pcr, pys, pyr, pzs, pzr,
):
    place, c = lax.axis_index("expert"), lax.axis_index("tensor")
    z, y = place // 2, place % 2
    rows, width = tokens_ref.shape
    units = gate_ref.shape[0]
    each = units // held
    to_core = {"tensor": 1 - c}
    to_y = {"expert": z * 2 + 1 - y}

    def remote(src, dst, send, recv, device):
        return pltpu.make_async_remote_copy(
            src_ref=src, dst_ref=dst, send_sem=send, recv_sem=recv,
            device_id=device, device_id_type=MESH,
        )

    barrier = pltpu.get_barrier_semaphore()
    pl.semaphore_signal(barrier, inc=1, device_id=to_core, device_id_type=MESH)
    pl.semaphore_signal(barrier, inc=1, device_id=to_y, device_id_type=MESH)
    for d in range(1, line):
        pl.semaphore_signal(
            barrier, inc=1, device_id={"expert": nearest(z, d) * 2 + y}, device_id_type=MESH
        )

    own = pltpu.make_async_copy(tokens_ref, tok.at[z, c, y, :, pl.ds(0, width)], own_sem)
    own.start()
    loads = []
    half = units // 2
    for number, (src, dst) in enumerate(((gate_ref, gate), (up_ref, up), (down_ref, down))):
        loads.append(pltpu.make_async_copy(src, dst, weight_sem.at[number]))
        loads[-1].start()

    lane = lax.broadcasted_iota(jnp.int32, (rows, EXTRA), 1)
    dense = jnp.zeros((rows, EXTRA), jnp.float32)
    for k in range(ids_ref.shape[1]):
        dense += jnp.where(ids_ref[:, k : k + 1] == lane % 32, route_ref[:, k : k + 1], 0.0)
    high = dense.astype(jnp.bfloat16).astype(jnp.float32)
    middle = (dense - high).astype(jnp.bfloat16).astype(jnp.float32)
    low = dense - high - middle
    terms = jnp.where(lane < 32, high, jnp.where(lane < 64, middle, low))
    tok[z, c, y, :, pl.ds(width, EXTRA)] = terms.astype(jnp.bfloat16)
    own.wait()
    pl.semaphore_wait(barrier, line + 1)

    def z_send(d):
        block = tok.at[z, c, y]
        return remote(block, block, zs.at[d], zr.at[z], {"expert": nearest(z, d) * 2 + y})

    def z_arrival(at):
        block = tok.at[at, c, y]
        return remote(block, block, zs.at[0], zr.at[at], to_y)

    def y_send(at):
        block = tok.at[at, c, y]
        return remote(block, block, ys.at[at], yr.at[at], to_y)

    def y_arrival(at):
        block = tok.at[at, c, 1 - y]
        return remote(block, block, ys.at[at], yr.at[at], to_y)

    def c_send(at, row):
        block = tok.at[at, c, row]
        return remote(block, block, cs.at[at, row], cr.at[at, row], to_core)

    def c_arrival(at, row):
        block = tok.at[at, 1 - c, row]
        return remote(block, block, cs.at[at, row], cr.at[at, row], to_core)

    y_send(z).start()
    for d in range(1, line):
        z_send(d).start()
    c_send(z, y).start()

    def arrive_first(step):
        at = nearest(z, step)
        z_arrival(at).wait_recv()
        y_send(at).start()
        c_send(at, y).start()

    def arrive_second(step):
        at = nearest(z, step)
        y_arrival(at).wait_recv()
        c_send(at, 1 - y).start()
        c_arrival(at, y).wait_recv()
        c_arrival(at, 1 - y).wait_recv()

    def part_core(step):
        at = nearest(z, step)
        return remote(
            part.at[step % 2, 1 - c], from_core.at[at], pcs.at[step], pcr.at[step], to_core
        )

    def part_y(step):
        at = nearest(z, step)
        return remote(
            part.at[step % 2, c, 1 - y], from_y.at[at], pys.at[step], pyr.at[step], to_y
        )

    def part_z(step):
        at = nearest(z, step)
        return remote(
            from_y.at[at], from_z.at[z], pzs.at[step], pzr.at[z], {"expert": at * 2 + y}
        )

    def add_core(step):
        at = nearest(z, step)
        part_core(step).wait_recv()
        for row in range(2):
            mine = part[step % 2, c, row].astype(jnp.float32)
            part[step % 2, c, row] = (mine + from_core[at, row].astype(jnp.float32)).astype(
                jnp.bfloat16
            )
        part_y(step).start()

    def add_y(step):
        at = nearest(z, step)
        part_y(step).wait_recv()
        mine = part[step % 2, c, y].astype(jnp.float32)
        from_y[at] = (mine + from_y[at].astype(jnp.float32)).astype(jnp.bfloat16)

        @pl.when(step > 0)
        def _():
            part_z(step).start()

    first = place * held

    def work(step, carry):
        at = nearest(z, step)

        @pl.when(step < line - 1)
        def _():
            arrive_first(step + 1)

        arrive_second(step)

        @pl.when(step == 0)
        def _():
            loads[0].wait()
            loads[1].wait()

        def hidden_tile(j, carry):
            start = pl.multiple_of(j * HID_TILE, HID_TILE)
            x = tok[at, :, :, :, pl.ds(0, width)].reshape(4 * rows, width)
            terms = tok[at, :, :, :, pl.ds(width, EXTRA)].reshape(4 * rows, EXTRA)
            transposed = (((1,), (1,)), ((), ()))
            g = lax.dot_general(
                x, gate[pl.ds(start, HID_TILE), :], transposed,
                preferred_element_type=jnp.float32,
            )
            u = lax.dot_general(
                x, up[pl.ds(start, HID_TILE), :], transposed,
                preferred_element_type=jnp.float32,
            )
            source = lax.broadcasted_iota(jnp.int32, (EXTRA, HID_TILE), 0)
            unit = start + lax.broadcasted_iota(jnp.int32, (EXTRA, HID_TILE), 1)
            expert = first
            for e in range(1, held):
                expert = expert + (unit >= e * each).astype(jnp.int32)
            chosen = jnp.where((source % 32 == expert) & (source < 96), 1.0, 0.0)
            weight = jnp.dot(
                terms, chosen.astype(jnp.bfloat16), preferred_element_type=jnp.float32
            )
            value = g / (1.0 + jnp.exp(-g)) * u * weight
            hid[:, pl.ds(start, HID_TILE)] = value.astype(jnp.bfloat16)
            return carry

        lax.fori_loop(0, units // HID_TILE, hidden_tile, 0)

        @pl.when(step > 0)
        def _():
            add_core(step - 1)

        @pl.when(step == 0)
        def _():
            loads[2].wait()

        @pl.when(step > 1)
        def _():
            part_core(step - 2).wait_send()
            part_y(step - 2).wait_send()

        def out_tile(j, carry):
            cols = pl.ds(pl.multiple_of(j * OUT_TILE, OUT_TILE), OUT_TILE)
            total = jnp.dot(hid[...], down[:, cols], preferred_element_type=jnp.float32)
            part[step % 2, :, :, :, cols] = total.astype(jnp.bfloat16).reshape(
                2, 2, rows, OUT_TILE
            )
            return carry

        lax.fori_loop(0, width // OUT_TILE, out_tile, 0)
        part_core(step).start()

        @pl.when(step > 0)
        def _():
            add_y(step - 1)

        return carry

    lax.fori_loop(0, line, work, 0)
    add_core(line - 1)
    add_y(line - 1)

    total = from_y[z].astype(jnp.float32)
    for d in range(1, line):
        at = nearest(z, d)
        remote(from_y.at[at], from_z.at[at], pzs.at[d], pzr.at[at], to_y).wait_recv()
        total += from_z[at].astype(jnp.float32)
    out_ref[...] = total.astype(out_ref.dtype)

    for d in range(1, line):
        z_send(d).wait_send()
        part_z(d).wait_send()
    for at in range(line):
        y_send(at).wait_send()
        for row in range(2):
            c_send(at, row).wait_send()
    for step in range(line - 2, line):
        part_core(step).wait_send()
        part_y(step).wait_send()


def in_one_kernel(tokens, expert_ids, route_weights, gate_weight, up_weight, down_weight):
    rows, width = tokens.shape
    line = lax.axis_size("expert") // 2
    held, each, _ = gate_weight.shape
    units = held * each
    bf16 = jnp.bfloat16
    dma = pltpu.SemaphoreType.DMA
    vmem = pl.BlockSpec(memory_space=pltpu.VMEM)
    hbm = pl.BlockSpec(memory_space=pl.ANY)
    flat = (units, width)
    group_rows = line * 4 * rows
    return pl.pallas_call(
        functools.partial(kernel, line, held),
        out_shape=jax.ShapeDtypeStruct((rows, width), bf16),
        in_specs=[hbm, vmem, vmem, hbm, hbm, hbm],
        out_specs=vmem,
        scratch_shapes=[
            pltpu.VMEM((line, 2, 2, rows, width + EXTRA), bf16),
            pltpu.VMEM(flat, bf16),
            pltpu.VMEM(flat, bf16),
            pltpu.VMEM(flat, bf16),
            pltpu.VMEM((4 * rows, units), bf16),
            pltpu.VMEM((2, 2, 2, rows, width), bf16),
            pltpu.VMEM((line, 2, rows, width), bf16),
            pltpu.VMEM((line, rows, width), bf16),
            pltpu.VMEM((line, rows, width), bf16),
            dma((3,)),
            dma,
            dma((line,)),
            dma((line,)),
            dma((line,)),
            dma((line,)),
            dma((line, 2)),
            dma((line, 2)),
            dma((line,)),
            dma((line,)),
            dma((line,)),
            dma((line,)),
            dma((line,)),
            dma((line,)),
        ],
        compiler_params=pltpu.CompilerParams(
            collective_id=0, has_side_effects=True, vmem_limit_bytes=63 * 1024 * 1024
        ),
        cost_estimate=pl.CostEstimate(
            flops=6 * group_rows * units * width,
            bytes_accessed=6 * units * width,
            transcendentals=group_rows * units,
        ),
        name="experts",
    )(
        tokens, expert_ids, route_weights,
        gate_weight.reshape(flat), up_weight.reshape(flat), down_weight.reshape(flat),
    )


def in_steps(tokens, expert_ids, route_weights, gate_weight, up_weight, down_weight):
    held = gate_weight.shape[0]
    experts = held * lax.axis_size("expert")
    labels = jnp.arange(experts, dtype=jnp.int32)
    named = expert_ids[:, :, None] == labels[None, None, :]
    weights = jnp.sum(jnp.where(named, route_weights[:, :, None], 0.0), axis=1)
    group = ("expert", "tensor")
    rows = lax.all_gather(tokens, group, axis=0, tiled=True)
    all_weights = lax.all_gather(weights, group, axis=0, tiled=True)
    first = lax.axis_index("expert") * held
    mine = lax.dynamic_slice_in_dim(all_weights, first, held, axis=1)
    total, hidden_units = rows.shape[0], gate_weight.shape[1]
    flat = (held * hidden_units, gate_weight.shape[2])
    transposed = (((1,), (1,)), ((), ()))
    gate = lax.dot_general(
        rows, gate_weight.reshape(flat), transposed, preferred_element_type=jnp.float32
    )
    up = lax.dot_general(
        rows, up_weight.reshape(flat), transposed, preferred_element_type=jnp.float32
    )
    scaled = (jax.nn.silu(gate) * up).reshape(total, held, hidden_units) * mine[:, :, None]
    hidden = scaled.reshape(total, held * hidden_units).astype(jnp.bfloat16)
    partial = jnp.dot(hidden, down_weight.reshape(flat), preferred_element_type=jnp.float32)
    return lax.psum_scatter(
        partial.astype(jnp.bfloat16), group, scatter_dimension=0, tiled=True
    )


def solution(mesh):
    spread = P(("groups", "expert", "tensor"), None)
    weight = P("expert", "tensor", None)
    small = mesh.shape["expert"] == 8 and mesh.shape["tensor"] == 2
    return jax.shard_map(
        in_one_kernel if small else in_steps,
        mesh=mesh,
        in_specs=(spread,) * 3 + (weight,) * 3,
        out_specs=spread,
        check_vma=False,
    )
```

```python
import functools

import jax
import jax.numpy as jnp
from jax import lax
from jax.experimental import pallas as pl
from jax.experimental.pallas import tpu as pltpu
from jax.sharding import PartitionSpec as P

MESH = pl.DeviceIdType.MESH
EXTRA = 128
HID_TILE = 256
OUT_TILE = 512
HALVES = 2


def nearest(z, step):
    lower = 1 - z // 2
    edge = z * lower + (3 - z) * (1 - lower)
    near = step + edge * (1 - step // 2) * (1 - 2 * (step % 2))
    return near * lower + (3 - near) * (1 - lower)


def slot(step):
    return step - 2 * (step // 3)


def kernel(
    line, held, tokens_ref, ids_ref, route_ref, gate_ref, up_ref, down_ref, out_ref,
    tok, gate, up, down, hid, part, from_core, from_y, from_z,
    weight_sem, own_sem, zs, zr, ys, yr, cs, cr, pcs, pcr, pys, pyr, pzs, pzr,
):
    place, c = lax.axis_index("expert"), lax.axis_index("tensor")
    z, y = place // 2, place % 2
    rows, width = tokens_ref.shape
    units = gate_ref.shape[0]
    each = units // held
    to_core = {"tensor": 1 - c}
    to_y = {"expert": z * 2 + 1 - y}

    def remote(src, dst, send, recv, device):
        return pltpu.make_async_remote_copy(
            src_ref=src, dst_ref=dst, send_sem=send, recv_sem=recv,
            device_id=device, device_id_type=MESH,
        )

    barrier = pltpu.get_barrier_semaphore()
    pl.semaphore_signal(barrier, inc=1, device_id=to_core, device_id_type=MESH)
    pl.semaphore_signal(barrier, inc=1, device_id=to_y, device_id_type=MESH)
    for d in range(1, line):
        pl.semaphore_signal(
            barrier, inc=1, device_id={"expert": nearest(z, d) * 2 + y}, device_id_type=MESH
        )

    own = pltpu.make_async_copy(tokens_ref, tok.at[z, c, y, :, pl.ds(0, width)], own_sem)
    own.start()
    loads = []
    for number, (src, dst) in enumerate(((gate_ref, gate), (up_ref, up), (down_ref, down))):
        loads.append(pltpu.make_async_copy(src, dst, weight_sem.at[number]))
        loads[-1].start()

    lane = lax.broadcasted_iota(jnp.int32, (rows, EXTRA), 1)
    dense = jnp.zeros((rows, EXTRA), jnp.float32)
    for k in range(ids_ref.shape[1]):
        dense += jnp.where(ids_ref[:, k : k + 1] == lane % 32, route_ref[:, k : k + 1], 0.0)
    high = dense.astype(jnp.bfloat16).astype(jnp.float32)
    middle = (dense - high).astype(jnp.bfloat16).astype(jnp.float32)
    low = dense - high - middle
    terms = jnp.where(lane < 32, high, jnp.where(lane < 64, middle, low))
    tok[z, c, y, :, pl.ds(width, EXTRA)] = terms.astype(jnp.bfloat16)
    own.wait()
    pl.semaphore_wait(barrier, line + 1)

    def z_hop(at, up_line):
        block = tok.at[at, c, y]
        side = 1 if up_line else 0
        there = (z + 2 * side - 1) * 2 + y
        return remote(block, block, zs.at[at, side], zr.at[at], {"expert": there})

    def z_arrival(at):
        block = tok.at[at, c, y]
        return remote(block, block, zs.at[at, 0], zr.at[at], to_y)

    def y_send(at):
        block = tok.at[at, c, y]
        return remote(block, block, ys.at[at], yr.at[at], to_y)

    def y_arrival(at):
        block = tok.at[at, c, 1 - y]
        return remote(block, block, ys.at[at], yr.at[at], to_y)

    def c_send(at, row):
        block = tok.at[at, c, row]
        return remote(block, block, cs.at[at, row], cr.at[at, row], to_core)

    def c_arrival(at, row):
        block = tok.at[at, 1 - c, row]
        return remote(block, block, cs.at[at, row], cr.at[at, row], to_core)

    @pl.when(z < line - 1)
    def _():
        z_hop(z, True).start()

    @pl.when(z > 0)
    def _():
        z_hop(z, False).start()

    y_send(z).start()
    c_send(z, y).start()

    def chain(far):
        @pl.when(z >= far)
        def _():
            at = z - far
            z_arrival(at).wait_recv()

            @pl.when(z < line - 1)
            def _():
                z_hop(at, True).start()

            y_send(at).start()
            c_send(at, y).start()

        @pl.when(z + far < line)
        def _():
            at = z + far
            z_arrival(at).wait_recv()

            @pl.when(z > 0)
            def _():
                z_hop(at, False).start()

            y_send(at).start()
            c_send(at, y).start()

    def arrive(step):
        at = nearest(z, step)
        y_arrival(at).wait_recv()
        c_send(at, 1 - y).start()
        c_arrival(at, y).wait_recv()
        c_arrival(at, 1 - y).wait_recv()

    def part_core(step, h):
        at = nearest(z, step)
        return remote(
            part.at[slot(step), h, 1 - c], from_core.at[at, h],
            pcs.at[step, h], pcr.at[step, h], to_core,
        )

    def part_y(step, h):
        at = nearest(z, step)
        return remote(
            part.at[slot(step), h, c, 1 - y], from_y.at[at, h],
            pys.at[step, h], pyr.at[step, h], to_y,
        )

    def part_z(step, h):
        at = nearest(z, step)
        return remote(
            from_y.at[at, h], from_z.at[z, h],
            pzs.at[step, h], pzr.at[z, h], {"expert": at * 2 + y},
        )

    def add_core(step, h):
        at = nearest(z, step)
        part_core(step, h).wait_recv()
        for row in (1 - y, y):
            mine = part[slot(step), h, c, row].astype(jnp.float32)
            part[slot(step), h, c, row] = (
                mine + from_core[at, h, row].astype(jnp.float32)
            ).astype(jnp.bfloat16)
        part_y(step, h).start()

    def add_y(step, h):
        at = nearest(z, step)
        part_y(step, h).wait_recv()
        mine = part[slot(step), h, c, y].astype(jnp.float32)
        from_y[at, h] = (mine + from_y[at, h].astype(jnp.float32)).astype(jnp.bfloat16)

    first = place * held
    span = width // HALVES
    chain(1)

    def work(step, carry):
        at = nearest(z, step)
        arrive(step)

        @pl.when(step == 0)
        def _():
            loads[0].wait()
            loads[1].wait()

        def hidden_tile(j, carry):
            start = pl.multiple_of(j * HID_TILE, HID_TILE)
            x = tok[at, :, :, :, pl.ds(0, width)].reshape(4 * rows, width)
            terms = tok[at, :, :, :, pl.ds(width, EXTRA)].reshape(4 * rows, EXTRA)
            transposed = (((1,), (1,)), ((), ()))
            g = lax.dot_general(
                x, gate[pl.ds(start, HID_TILE), :], transposed,
                preferred_element_type=jnp.float32,
            )
            u = lax.dot_general(
                x, up[pl.ds(start, HID_TILE), :], transposed,
                preferred_element_type=jnp.float32,
            )
            source = lax.broadcasted_iota(jnp.int32, (EXTRA, HID_TILE), 0)
            unit = start + lax.broadcasted_iota(jnp.int32, (EXTRA, HID_TILE), 1)
            expert = first
            for e in range(1, held):
                expert = expert + (unit >= e * each).astype(jnp.int32)
            chosen = jnp.where((source % 32 == expert) & (source < 96), 1.0, 0.0)
            weight = jnp.dot(
                terms, chosen.astype(jnp.bfloat16), preferred_element_type=jnp.float32
            )
            value = g / (1.0 + jnp.exp(-g)) * u * weight
            hid[:, pl.ds(start, HID_TILE)] = value.astype(jnp.bfloat16)
            return carry

        lax.fori_loop(0, units // HID_TILE, hidden_tile, 0)

        for far in range(2, line):
            @pl.when(step == far - 2)
            def _():
                chain(far)

        @pl.when(step == 0)
        def _():
            loads[2].wait()

        @pl.when(step == 3)
        def _():
            for h in range(HALVES):
                part_core(step - 2, h).wait_send()
                part_y(step - 2, h).wait_send()

        for h in range(HALVES):
            def out_tile(j, carry):
                inner = pl.ds(pl.multiple_of(j * OUT_TILE, OUT_TILE), OUT_TILE)
                cols = pl.ds(pl.multiple_of(h * span + j * OUT_TILE, OUT_TILE), OUT_TILE)
                total = jnp.dot(hid[...], down[:, cols], preferred_element_type=jnp.float32)
                part[slot(step), h, :, :, :, inner] = total.astype(jnp.bfloat16).reshape(
                    2, 2, rows, OUT_TILE
                )
                return carry

            lax.fori_loop(0, span // OUT_TILE, out_tile, 0)
            part_core(step, h).start()
            if h > 0:
                @pl.when(step > 0)
                def _():
                    add_core(step, h - 1)

        @pl.when(step > 0)
        def _():
            add_core(step, HALVES - 1)

        @pl.when(step > 1)
        def _():
            for h in range(HALVES):
                add_y(step - 1, h)
                part_z(step - 1, h).start()

        return carry

    lax.fori_loop(0, line, work, 0)
    for h in range(HALVES):
        add_core(0, h)
    for h in range(HALVES):
        add_y(line - 1, h)
        part_z(line - 1, h).start()

    for h in range(HALVES):
        add_y(0, h)
        total = from_y[z, h].astype(jnp.float32)
        for d in range(1, line):
            at = nearest(z, d)
            remote(
                from_y.at[at, h], from_z.at[at, h], pzs.at[d, h], pzr.at[at, h], to_y
            ).wait_recv()
            total += from_z[at, h].astype(jnp.float32)
        out_ref[:, pl.ds(h * span, span)] = total.astype(out_ref.dtype)

    for at in range(line):
        @pl.when((at <= z) & (z < line - 1))
        def _():
            z_hop(at, True).wait_send()

        @pl.when((at >= z) & (z > 0))
        def _():
            z_hop(at, False).wait_send()

        y_send(at).wait_send()
        for row in range(2):
            c_send(at, row).wait_send()
    for h in range(HALVES):
        for d in range(1, line):
            part_z(d, h).wait_send()
        for step in (0, 2, 3):
            part_core(step, h).wait_send()
            part_y(step, h).wait_send()


def in_one_kernel(tokens, expert_ids, route_weights, gate_weight, up_weight, down_weight):
    rows, width = tokens.shape
    line = lax.axis_size("expert") // 2
    held, each, _ = gate_weight.shape
    units = held * each
    bf16 = jnp.bfloat16
    dma = pltpu.SemaphoreType.DMA
    vmem = pl.BlockSpec(memory_space=pltpu.VMEM)
    hbm = pl.BlockSpec(memory_space=pl.ANY)
    flat = (units, width)
    group_rows = line * 4 * rows
    return pl.pallas_call(
        functools.partial(kernel, line, held),
        out_shape=jax.ShapeDtypeStruct((rows, width), bf16),
        in_specs=[hbm, vmem, vmem, hbm, hbm, hbm],
        out_specs=vmem,
        scratch_shapes=[
            pltpu.VMEM((line, 2, 2, rows, width + EXTRA), bf16),
            pltpu.VMEM(flat, bf16),
            pltpu.VMEM(flat, bf16),
            pltpu.VMEM(flat, bf16),
            pltpu.VMEM((4 * rows, units), bf16),
            pltpu.VMEM((3, HALVES, 2, 2, rows, width // HALVES), bf16),
            pltpu.VMEM((line, HALVES, 2, rows, width // HALVES), bf16),
            pltpu.VMEM((line, HALVES, rows, width // HALVES), bf16),
            pltpu.VMEM((line, HALVES, rows, width // HALVES), bf16),
            dma((3,)),
            dma,
            dma((line, 2)),
            dma((line,)),
            dma((line,)),
            dma((line,)),
            dma((line, 2)),
            dma((line, 2)),
            dma((line, HALVES)),
            dma((line, HALVES)),
            dma((line, HALVES)),
            dma((line, HALVES)),
            dma((line, HALVES)),
            dma((line, HALVES)),
        ],
        compiler_params=pltpu.CompilerParams(
            collective_id=0, has_side_effects=True, vmem_limit_bytes=63 * 1024 * 1024
        ),
        cost_estimate=pl.CostEstimate(
            flops=6 * group_rows * units * width,
            bytes_accessed=6 * units * width,
            transcendentals=group_rows * units,
        ),
        name="experts",
    )(
        tokens, expert_ids, route_weights,
        gate_weight.reshape(flat), up_weight.reshape(flat), down_weight.reshape(flat),
    )


def in_steps(tokens, expert_ids, route_weights, gate_weight, up_weight, down_weight):
    held = gate_weight.shape[0]
    experts = held * lax.axis_size("expert")
    labels = jnp.arange(experts, dtype=jnp.int32)
    named = expert_ids[:, :, None] == labels[None, None, :]
    weights = jnp.sum(jnp.where(named, route_weights[:, :, None], 0.0), axis=1)
    group = ("expert", "tensor")
    rows = lax.all_gather(tokens, group, axis=0, tiled=True)
    all_weights = lax.all_gather(weights, group, axis=0, tiled=True)
    first = lax.axis_index("expert") * held
    mine = lax.dynamic_slice_in_dim(all_weights, first, held, axis=1)
    total, hidden_units = rows.shape[0], gate_weight.shape[1]
    flat = (held * hidden_units, gate_weight.shape[2])
    transposed = (((1,), (1,)), ((), ()))
    gate = lax.dot_general(
        rows, gate_weight.reshape(flat), transposed, preferred_element_type=jnp.float32
    )
    up = lax.dot_general(
        rows, up_weight.reshape(flat), transposed, preferred_element_type=jnp.float32
    )
    scaled = (jax.nn.silu(gate) * up).reshape(total, held, hidden_units) * mine[:, :, None]
    hidden = scaled.reshape(total, held * hidden_units).astype(jnp.bfloat16)
    partial = jnp.dot(hidden, down_weight.reshape(flat), preferred_element_type=jnp.float32)
    return lax.psum_scatter(
        partial.astype(jnp.bfloat16), group, scatter_dimension=0, tiled=True
    )


def solution(mesh):
    spread = P(("groups", "expert", "tensor"), None)
    weight = P("expert", "tensor", None)
    small = mesh.shape["expert"] == 8 and mesh.shape["tensor"] == 2
    return jax.shard_map(
        in_one_kernel if small else in_steps,
        mesh=mesh,
        in_specs=(spread,) * 3 + (weight,) * 3,
        out_specs=spread,
        check_vma=False,
    )
```

```python
import functools

import jax
import jax.numpy as jnp
from jax import lax
from jax.experimental import pallas as pl
from jax.experimental.pallas import tpu as pltpu
from jax.sharding import PartitionSpec as P

MESH = pl.DeviceIdType.MESH
EXTRA = 128
HID_TILE = 256
OUT_TILE = 512
HALVES = 2


def nearest(z, step):
    lower = 1 - z // 2
    edge = z * lower + (3 - z) * (1 - lower)
    near = step + edge * (1 - step // 2) * (1 - 2 * (step % 2))
    return near * lower + (3 - near) * (1 - lower)


def slot(step):
    return step - 2 * (step // 3)


def kernel(
    line, held, tokens_ref, ids_ref, route_ref, gate_ref, up_ref, down_ref, out_ref,
    tok, gate, up, down, hid, part, from_core, from_y, from_z,
    weight_sem, own_sem, zs, zr, ys, yr, cs, cr, pcs, pcr, pys, pyr, pzs, pzr,
):
    place, c = lax.axis_index("expert"), lax.axis_index("tensor")
    z, y = place // 2, place % 2
    rows, width = tokens_ref.shape
    units = gate_ref.shape[0]
    each = units // held
    to_core = {"tensor": 1 - c}
    to_y = {"expert": z * 2 + 1 - y}

    def remote(src, dst, send, recv, device):
        return pltpu.make_async_remote_copy(
            src_ref=src, dst_ref=dst, send_sem=send, recv_sem=recv,
            device_id=device, device_id_type=MESH,
        )

    barrier = pltpu.get_barrier_semaphore()
    pl.semaphore_signal(barrier, inc=1, device_id=to_core, device_id_type=MESH)
    pl.semaphore_signal(barrier, inc=1, device_id=to_y, device_id_type=MESH)
    for d in range(1, line):
        pl.semaphore_signal(
            barrier, inc=1, device_id={"expert": nearest(z, d) * 2 + y}, device_id_type=MESH
        )

    own = pltpu.make_async_copy(tokens_ref, tok.at[z, c, y, :, pl.ds(0, width)], own_sem)
    own.start()
    loads = []
    for number, (src, dst) in enumerate(((gate_ref, gate), (up_ref, up), (down_ref, down))):
        loads.append(pltpu.make_async_copy(src, dst, weight_sem.at[number]))
        loads[-1].start()

    lane = lax.broadcasted_iota(jnp.int32, (rows, EXTRA), 1)
    dense = jnp.zeros((rows, EXTRA), jnp.float32)
    for k in range(ids_ref.shape[1]):
        dense += jnp.where(ids_ref[:, k : k + 1] == lane % 32, route_ref[:, k : k + 1], 0.0)
    high = dense.astype(jnp.bfloat16).astype(jnp.float32)
    middle = (dense - high).astype(jnp.bfloat16).astype(jnp.float32)
    low = dense - high - middle
    terms = jnp.where(lane < 32, high, jnp.where(lane < 64, middle, low))
    tok[z, c, y, :, pl.ds(width, EXTRA)] = terms.astype(jnp.bfloat16)
    own.wait()
    pl.semaphore_wait(barrier, line + 1)

    def z_hop(at, up_line):
        block = tok.at[at, c, y]
        side = 1 if up_line else 0
        there = (z + 2 * side - 1) * 2 + y
        return remote(block, block, zs.at[at, side], zr.at[at], {"expert": there})

    def z_arrival(at):
        block = tok.at[at, c, y]
        return remote(block, block, zs.at[at, 0], zr.at[at], to_y)

    def y_send(at):
        block = tok.at[at, c, y]
        return remote(block, block, ys.at[at], yr.at[at], to_y)

    def y_arrival(at):
        block = tok.at[at, c, 1 - y]
        return remote(block, block, ys.at[at], yr.at[at], to_y)

    def c_send(at, row):
        block = tok.at[at, c, row]
        return remote(block, block, cs.at[at, row], cr.at[at, row], to_core)

    def c_arrival(at, row):
        block = tok.at[at, 1 - c, row]
        return remote(block, block, cs.at[at, row], cr.at[at, row], to_core)

    @pl.when(z < line - 1)
    def _():
        z_hop(z, True).start()

    @pl.when(z > 0)
    def _():
        z_hop(z, False).start()

    y_send(z).start()
    c_send(z, y).start()

    def chain(far):
        @pl.when(z >= far)
        def _():
            at = z - far
            z_arrival(at).wait_recv()

            @pl.when(z < line - 1)
            def _():
                z_hop(at, True).start()

            y_send(at).start()
            c_send(at, y).start()

        @pl.when(z + far < line)
        def _():
            at = z + far
            z_arrival(at).wait_recv()

            @pl.when(z > 0)
            def _():
                z_hop(at, False).start()

            y_send(at).start()
            c_send(at, y).start()

    def arrive(step):
        at = nearest(z, step)
        y_arrival(at).wait_recv()
        c_send(at, 1 - y).start()
        c_arrival(at, y).wait_recv()
        c_arrival(at, 1 - y).wait_recv()

    def part_core(step, h):
        at = nearest(z, step)
        return remote(
            part.at[slot(step), h, 1 - c], from_core.at[at, h],
            pcs.at[step, h], pcr.at[step, h], to_core,
        )

    def part_y(step, h):
        at = nearest(z, step)
        return remote(
            part.at[slot(step), h, c, 1 - y], from_y.at[at, h],
            pys.at[step, h], pyr.at[step, h], to_y,
        )

    middle = (z > 0) & (z < line - 1)

    def sum_send(step, h, up_line):
        at = nearest(z, step)
        there = z + 1 if up_line else z - 1
        place_there = at if up_line else at + (line - at) * (1 - (z - 1 - at + line - 1) // line)
        return remote(
            from_y.at[at, h], from_z.at[place_there, h],
            pzs.at[step, h], pzr.at[place_there, h], {"expert": there * 2 + y},
        )

    def sum_arrival(at, h):
        return remote(from_y.at[z, h], from_z.at[at, h], pzs.at[0, h], pzr.at[at, h], to_y)

    def pass_on(step, h):
        at = nearest(z, step)

        @pl.when(middle)
        def _():
            sum_arrival(at, h).wait_recv()
            mine = from_y[at, h].astype(jnp.float32)
            from_y[at, h] = (mine + from_z[at, h].astype(jnp.float32)).astype(jnp.bfloat16)

        @pl.when(at > z)
        def _():
            sum_send(step, h, True).start()

        @pl.when(at < z)
        def _():
            sum_send(step, h, False).start()

    def add_core(step, h):
        at = nearest(z, step)
        part_core(step, h).wait_recv()
        for row in (1 - y, y):
            mine = part[slot(step), h, c, row].astype(jnp.float32)
            part[slot(step), h, c, row] = (
                mine + from_core[at, h, row].astype(jnp.float32)
            ).astype(jnp.bfloat16)
        part_y(step, h).start()

    def add_y(step, h):
        at = nearest(z, step)
        part_y(step, h).wait_recv()
        mine = part[slot(step), h, c, y].astype(jnp.float32)
        from_y[at, h] = (mine + from_y[at, h].astype(jnp.float32)).astype(jnp.bfloat16)

    first = place * held
    span = width // HALVES
    chain(1)

    def work(step, carry):
        at = nearest(z, step)
        arrive(step)

        @pl.when(step == 0)
        def _():
            loads[0].wait()
            loads[1].wait()

        def hidden_tile(j, carry):
            start = pl.multiple_of(j * HID_TILE, HID_TILE)
            x = tok[at, :, :, :, pl.ds(0, width)].reshape(4 * rows, width)
            terms = tok[at, :, :, :, pl.ds(width, EXTRA)].reshape(4 * rows, EXTRA)
            transposed = (((1,), (1,)), ((), ()))
            g = lax.dot_general(
                x, gate[pl.ds(start, HID_TILE), :], transposed,
                preferred_element_type=jnp.float32,
            )
            u = lax.dot_general(
                x, up[pl.ds(start, HID_TILE), :], transposed,
                preferred_element_type=jnp.float32,
            )
            source = lax.broadcasted_iota(jnp.int32, (EXTRA, HID_TILE), 0)
            unit = start + lax.broadcasted_iota(jnp.int32, (EXTRA, HID_TILE), 1)
            expert = first
            for e in range(1, held):
                expert = expert + (unit >= e * each).astype(jnp.int32)
            chosen = jnp.where((source % 32 == expert) & (source < 96), 1.0, 0.0)
            weight = jnp.dot(
                terms, chosen.astype(jnp.bfloat16), preferred_element_type=jnp.float32
            )
            value = g / (1.0 + jnp.exp(-g)) * u * weight
            hid[:, pl.ds(start, HID_TILE)] = value.astype(jnp.bfloat16)
            return carry

        lax.fori_loop(0, units // HID_TILE, hidden_tile, 0)

        for far in range(2, line):
            @pl.when(step == far - 2)
            def _():
                chain(far)

        @pl.when(step == 0)
        def _():
            loads[2].wait()

        @pl.when(step == 3)
        def _():
            for h in range(HALVES):
                part_core(step - 2, h).wait_send()
                part_y(step - 2, h).wait_send()

        for h in range(HALVES):
            def out_tile(j, carry):
                inner = pl.ds(pl.multiple_of(j * OUT_TILE, OUT_TILE), OUT_TILE)
                cols = pl.ds(pl.multiple_of(h * span + j * OUT_TILE, OUT_TILE), OUT_TILE)
                total = jnp.dot(hid[...], down[:, cols], preferred_element_type=jnp.float32)
                part[slot(step), h, :, :, :, inner] = total.astype(jnp.bfloat16).reshape(
                    2, 2, rows, OUT_TILE
                )
                return carry

            lax.fori_loop(0, span // OUT_TILE, out_tile, 0)
            part_core(step, h).start()
            if h > 0:
                @pl.when(step > 0)
                def _():
                    add_core(step, h - 1)

        @pl.when(step > 0)
        def _():
            add_core(step, HALVES - 1)

        @pl.when(step > 1)
        def _():
            for h in range(HALVES):
                add_y(step - 1, h)

                @pl.when(jnp.logical_not(middle))
                def _():
                    pass_on(step - 1, h)

        return carry

    lax.fori_loop(0, line, work, 0)
    for h in range(HALVES):
        add_core(0, h)
    @pl.when(middle)
    def _():
        for h in range(HALVES):
            pass_on(line - 2, h)

    for h in range(HALVES):
        add_y(line - 1, h)
        pass_on(line - 1, h)

    @pl.when(middle)
    def _():
        for h in range(HALVES):
            pass_on(1, h)

    for h in range(HALVES):
        add_y(0, h)

        def finish(slots):
            total = from_y[z, h].astype(jnp.float32)
            for at in slots:
                sum_arrival(at, h).wait_recv()
                total += from_z[at, h].astype(jnp.float32)
            out_ref[:, pl.ds(h * span, span)] = total.astype(out_ref.dtype)

        @pl.when(z == 0)
        def _():
            finish((line,))

        @pl.when(middle)
        def _():
            finish((z, line))

        @pl.when(z == line - 1)
        def _():
            finish((z,))

    for at in range(line):
        @pl.when((at <= z) & (z < line - 1))
        def _():
            z_hop(at, True).wait_send()

        @pl.when((at >= z) & (z > 0))
        def _():
            z_hop(at, False).wait_send()

        y_send(at).wait_send()
        for row in range(2):
            c_send(at, row).wait_send()
    for h in range(HALVES):
        for d in range(1, line):
            remote(
                from_y.at[z, h], from_z.at[z, h], pzs.at[d, h], pzr.at[z, h], to_y
            ).wait_send()
        for step in (0, 2, 3):
            part_core(step, h).wait_send()
            part_y(step, h).wait_send()


def in_one_kernel(tokens, expert_ids, route_weights, gate_weight, up_weight, down_weight):
    rows, width = tokens.shape
    line = lax.axis_size("expert") // 2
    held, each, _ = gate_weight.shape
    units = held * each
    bf16 = jnp.bfloat16
    dma = pltpu.SemaphoreType.DMA
    vmem = pl.BlockSpec(memory_space=pltpu.VMEM)
    hbm = pl.BlockSpec(memory_space=pl.ANY)
    flat = (units, width)
    group_rows = line * 4 * rows
    return pl.pallas_call(
        functools.partial(kernel, line, held),
        out_shape=jax.ShapeDtypeStruct((rows, width), bf16),
        in_specs=[hbm, vmem, vmem, hbm, hbm, hbm],
        out_specs=vmem,
        scratch_shapes=[
            pltpu.VMEM((line, 2, 2, rows, width + EXTRA), bf16),
            pltpu.VMEM(flat, bf16),
            pltpu.VMEM(flat, bf16),
            pltpu.VMEM(flat, bf16),
            pltpu.VMEM((4 * rows, units), bf16),
            pltpu.VMEM((3, HALVES, 2, 2, rows, width // HALVES), bf16),
            pltpu.VMEM((line, HALVES, 2, rows, width // HALVES), bf16),
            pltpu.VMEM((line, HALVES, rows, width // HALVES), bf16),
            pltpu.VMEM((line + 1, HALVES, rows, width // HALVES), bf16),
            dma((3,)),
            dma,
            dma((line, 2)),
            dma((line,)),
            dma((line,)),
            dma((line,)),
            dma((line, 2)),
            dma((line, 2)),
            dma((line, HALVES)),
            dma((line, HALVES)),
            dma((line, HALVES)),
            dma((line, HALVES)),
            dma((line, HALVES)),
            dma((line + 1, HALVES)),
        ],
        compiler_params=pltpu.CompilerParams(
            collective_id=0, has_side_effects=True, vmem_limit_bytes=63 * 1024 * 1024
        ),
        cost_estimate=pl.CostEstimate(
            flops=6 * group_rows * units * width,
            bytes_accessed=6 * units * width,
            transcendentals=group_rows * units,
        ),
        name="experts",
    )(
        tokens, expert_ids, route_weights,
        gate_weight.reshape(flat), up_weight.reshape(flat), down_weight.reshape(flat),
    )


def in_steps(tokens, expert_ids, route_weights, gate_weight, up_weight, down_weight):
    held = gate_weight.shape[0]
    experts = held * lax.axis_size("expert")
    labels = jnp.arange(experts, dtype=jnp.int32)
    named = expert_ids[:, :, None] == labels[None, None, :]
    weights = jnp.sum(jnp.where(named, route_weights[:, :, None], 0.0), axis=1)
    group = ("expert", "tensor")
    rows = lax.all_gather(tokens, group, axis=0, tiled=True)
    all_weights = lax.all_gather(weights, group, axis=0, tiled=True)
    first = lax.axis_index("expert") * held
    mine = lax.dynamic_slice_in_dim(all_weights, first, held, axis=1)
    total, hidden_units = rows.shape[0], gate_weight.shape[1]
    flat = (held * hidden_units, gate_weight.shape[2])
    transposed = (((1,), (1,)), ((), ()))
    gate = lax.dot_general(
        rows, gate_weight.reshape(flat), transposed, preferred_element_type=jnp.float32
    )
    up = lax.dot_general(
        rows, up_weight.reshape(flat), transposed, preferred_element_type=jnp.float32
    )
    scaled = (jax.nn.silu(gate) * up).reshape(total, held, hidden_units) * mine[:, :, None]
    hidden = scaled.reshape(total, held * hidden_units).astype(jnp.bfloat16)
    partial = jnp.dot(hidden, down_weight.reshape(flat), preferred_element_type=jnp.float32)
    return lax.psum_scatter(
        partial.astype(jnp.bfloat16), group, scatter_dimension=0, tiled=True
    )


def solution(mesh):
    spread = P(("groups", "expert", "tensor"), None)
    weight = P("expert", "tensor", None)
    small = mesh.shape["expert"] == 8 and mesh.shape["tensor"] == 2
    return jax.shard_map(
        in_one_kernel if small else in_steps,
        mesh=mesh,
        in_specs=(spread,) * 3 + (weight,) * 3,
        out_specs=spread,
        check_vma=False,
    )
```

```python
import functools

import jax
import jax.numpy as jnp
from jax import lax
from jax.experimental import pallas as pl
from jax.experimental.pallas import tpu as pltpu
from jax.sharding import PartitionSpec as P

MESH = pl.DeviceIdType.MESH
EXTRA = 128
HID_TILE = 256
OUT_TILE = 512
PIECES = 4


def nearest(z, step):
    lower = 1 - z // 2
    edge = z * lower + (3 - z) * (1 - lower)
    near = step + edge * (1 - step // 2) * (1 - 2 * (step % 2))
    return near * lower + (3 - near) * (1 - lower)


def slot(step):
    return step - 2 * (step // 3)


def kernel(
    line, held, tokens_ref, ids_ref, route_ref, gate_ref, up_ref, down_ref, out_ref,
    tok, gate, up, down, hid, part, from_core, from_y, from_z,
    weight_sem, own_sem, zs, zr, ys, yr, cs, cr, pcs, pcr, pys, pyr, pzs, pzr,
):
    place, c = lax.axis_index("expert"), lax.axis_index("tensor")
    z, y = place // 2, place % 2
    rows, width = tokens_ref.shape
    units = gate_ref.shape[0]
    each = units // held
    to_core = {"tensor": 1 - c}
    to_y = {"expert": z * 2 + 1 - y}

    def remote(src, dst, send, recv, device):
        return pltpu.make_async_remote_copy(
            src_ref=src, dst_ref=dst, send_sem=send, recv_sem=recv,
            device_id=device, device_id_type=MESH,
        )

    barrier = pltpu.get_barrier_semaphore()
    pl.semaphore_signal(barrier, inc=1, device_id=to_core, device_id_type=MESH)
    pl.semaphore_signal(barrier, inc=1, device_id=to_y, device_id_type=MESH)
    for d in range(1, line):
        pl.semaphore_signal(
            barrier, inc=1, device_id={"expert": nearest(z, d) * 2 + y}, device_id_type=MESH
        )

    own = pltpu.make_async_copy(tokens_ref, tok.at[z, c, y, :, pl.ds(0, width)], own_sem)
    own.start()
    loads = []
    for number, (src, dst) in enumerate(((gate_ref, gate), (up_ref, up), (down_ref, down))):
        loads.append(pltpu.make_async_copy(src, dst, weight_sem.at[number]))
        loads[-1].start()

    lane = lax.broadcasted_iota(jnp.int32, (rows, EXTRA), 1)
    dense = jnp.zeros((rows, EXTRA), jnp.float32)
    for k in range(ids_ref.shape[1]):
        dense += jnp.where(ids_ref[:, k : k + 1] == lane % 32, route_ref[:, k : k + 1], 0.0)
    high = dense.astype(jnp.bfloat16).astype(jnp.float32)
    middle = (dense - high).astype(jnp.bfloat16).astype(jnp.float32)
    low = dense - high - middle
    terms = jnp.where(lane < 32, high, jnp.where(lane < 64, middle, low))
    tok[z, c, y, :, pl.ds(width, EXTRA)] = terms.astype(jnp.bfloat16)
    own.wait()
    pl.semaphore_wait(barrier, line + 1)

    def z_hop(at, up_line):
        block = tok.at[at, c, y]
        side = 1 if up_line else 0
        there = (z + 2 * side - 1) * 2 + y
        return remote(block, block, zs.at[at, side], zr.at[at], {"expert": there})

    def z_arrival(at):
        block = tok.at[at, c, y]
        return remote(block, block, zs.at[at, 0], zr.at[at], to_y)

    def y_send(at):
        block = tok.at[at, c, y]
        return remote(block, block, ys.at[at], yr.at[at], to_y)

    def y_arrival(at):
        block = tok.at[at, c, 1 - y]
        return remote(block, block, ys.at[at], yr.at[at], to_y)

    def c_send(at, row):
        block = tok.at[at, c, row]
        return remote(block, block, cs.at[at, row], cr.at[at, row], to_core)

    def c_arrival(at, row):
        block = tok.at[at, 1 - c, row]
        return remote(block, block, cs.at[at, row], cr.at[at, row], to_core)

    @pl.when(z < line - 1)
    def _():
        z_hop(z, True).start()

    @pl.when(z > 0)
    def _():
        z_hop(z, False).start()

    y_send(z).start()
    c_send(z, y).start()

    def chain(far):
        @pl.when(z >= far)
        def _():
            at = z - far
            z_arrival(at).wait_recv()

            @pl.when(z < line - 1)
            def _():
                z_hop(at, True).start()

            y_send(at).start()
            c_send(at, y).start()

        @pl.when(z + far < line)
        def _():
            at = z + far
            z_arrival(at).wait_recv()

            @pl.when(z > 0)
            def _():
                z_hop(at, False).start()

            y_send(at).start()
            c_send(at, y).start()

    def arrive(step):
        at = nearest(z, step)
        y_arrival(at).wait_recv()
        c_send(at, 1 - y).start()
        c_arrival(at, y).wait_recv()
        c_arrival(at, 1 - y).wait_recv()

    def part_core(step, h):
        at = nearest(z, step)
        return remote(
            part.at[slot(step), h, 1 - c], from_core.at[at, h],
            pcs.at[step, h], pcr.at[step, h], to_core,
        )

    def part_y(step, h):
        at = nearest(z, step)
        return remote(
            part.at[slot(step), h, c, 1 - y], from_y.at[at, h],
            pys.at[step, h], pyr.at[step, h], to_y,
        )

    middle = (z > 0) & (z < line - 1)

    def sum_send(step, h, up_line):
        at = nearest(z, step)
        there = z + 1 if up_line else z - 1
        place_there = at if up_line else at + (line - at) * (1 - (z - 1 - at + line - 1) // line)
        return remote(
            from_y.at[at, h], from_z.at[place_there, h],
            pzs.at[step, h], pzr.at[place_there, h], {"expert": there * 2 + y},
        )

    def sum_arrival(at, h):
        return remote(from_y.at[z, h], from_z.at[at, h], pzs.at[0, h], pzr.at[at, h], to_y)

    def pass_on(step, h):
        at = nearest(z, step)

        @pl.when(middle)
        def _():
            sum_arrival(at, h).wait_recv()
            mine = from_y[at, h].astype(jnp.float32)
            from_y[at, h] = (mine + from_z[at, h].astype(jnp.float32)).astype(jnp.bfloat16)

        @pl.when(at > z)
        def _():
            sum_send(step, h, True).start()

        @pl.when(at < z)
        def _():
            sum_send(step, h, False).start()

    def add_core(step, h):
        at = nearest(z, step)
        part_core(step, h).wait_recv()
        for row in (1 - y, y):
            mine = part[slot(step), h, c, row].astype(jnp.float32)
            part[slot(step), h, c, row] = (
                mine + from_core[at, h, row].astype(jnp.float32)
            ).astype(jnp.bfloat16)
        part_y(step, h).start()

    def add_y(step, h):
        at = nearest(z, step)
        part_y(step, h).wait_recv()
        mine = part[slot(step), h, c, y].astype(jnp.float32)
        from_y[at, h] = (mine + from_y[at, h].astype(jnp.float32)).astype(jnp.bfloat16)

    first = place * held
    span = width // PIECES
    chain(1)

    def work(step, carry):
        at = nearest(z, step)
        arrive(step)

        @pl.when(step == 0)
        def _():
            loads[0].wait()
            loads[1].wait()

        def hidden_tile(j, carry):
            start = pl.multiple_of(j * HID_TILE, HID_TILE)
            x = tok[at, :, :, :, pl.ds(0, width)].reshape(4 * rows, width)
            terms = tok[at, :, :, :, pl.ds(width, EXTRA)].reshape(4 * rows, EXTRA)
            transposed = (((1,), (1,)), ((), ()))
            g = lax.dot_general(
                x, gate[pl.ds(start, HID_TILE), :], transposed,
                preferred_element_type=jnp.float32,
            )
            u = lax.dot_general(
                x, up[pl.ds(start, HID_TILE), :], transposed,
                preferred_element_type=jnp.float32,
            )
            source = lax.broadcasted_iota(jnp.int32, (EXTRA, HID_TILE), 0)
            unit = start + lax.broadcasted_iota(jnp.int32, (EXTRA, HID_TILE), 1)
            expert = first
            for e in range(1, held):
                expert = expert + (unit >= e * each).astype(jnp.int32)
            chosen = jnp.where((source % 32 == expert) & (source < 96), 1.0, 0.0)
            weight = jnp.dot(
                terms, chosen.astype(jnp.bfloat16), preferred_element_type=jnp.float32
            )
            value = g / (1.0 + jnp.exp(-g)) * u * weight
            hid[:, pl.ds(start, HID_TILE)] = value.astype(jnp.bfloat16)
            return carry

        lax.fori_loop(0, units // HID_TILE, hidden_tile, 0)

        for far in range(2, line):
            @pl.when(step == far - 2)
            def _():
                chain(far)

        @pl.when(step == 0)
        def _():
            loads[2].wait()

        @pl.when(step == 3)
        def _():
            for h in range(PIECES):
                part_core(step - 2, h).wait_send()
                part_y(step - 2, h).wait_send()

        for h in range(PIECES):
            def out_tile(j, carry):
                inner = pl.ds(pl.multiple_of(j * OUT_TILE, OUT_TILE), OUT_TILE)
                cols = pl.ds(pl.multiple_of(h * span + j * OUT_TILE, OUT_TILE), OUT_TILE)
                total = jnp.dot(hid[...], down[:, cols], preferred_element_type=jnp.float32)
                part[slot(step), h, :, :, :, inner] = total.astype(jnp.bfloat16).reshape(
                    2, 2, rows, OUT_TILE
                )
                return carry

            lax.fori_loop(0, span // OUT_TILE, out_tile, 0)
            part_core(step, h).start()
            if h > 0:
                @pl.when(step > 0)
                def _():
                    add_core(step, h - 1)

        @pl.when(step > 0)
        def _():
            add_core(step, PIECES - 1)

        @pl.when(step > 1)
        def _():
            for h in range(PIECES):
                add_y(step - 1, h)

                @pl.when(jnp.logical_not(middle))
                def _():
                    pass_on(step - 1, h)

        return carry

    lax.fori_loop(0, line, work, 0)
    for h in range(PIECES):
        add_core(0, h)
    @pl.when(middle)
    def _():
        for h in range(PIECES):
            pass_on(line - 2, h)

    for h in range(PIECES):
        add_y(line - 1, h)
        pass_on(line - 1, h)

    @pl.when(middle)
    def _():
        for h in range(PIECES):
            pass_on(1, h)

    for h in range(PIECES):
        add_y(0, h)

        def finish(slots):
            total = from_y[z, h].astype(jnp.float32)
            for at in slots:
                sum_arrival(at, h).wait_recv()
                total += from_z[at, h].astype(jnp.float32)
            out_ref[:, pl.ds(h * span, span)] = total.astype(out_ref.dtype)

        @pl.when(z == 0)
        def _():
            finish((line,))

        @pl.when(middle)
        def _():
            finish((z, line))

        @pl.when(z == line - 1)
        def _():
            finish((z,))

    for at in range(line):
        @pl.when((at <= z) & (z < line - 1))
        def _():
            z_hop(at, True).wait_send()

        @pl.when((at >= z) & (z > 0))
        def _():
            z_hop(at, False).wait_send()

        y_send(at).wait_send()
        for row in range(2):
            c_send(at, row).wait_send()
    for h in range(PIECES):
        for d in range(1, line):
            remote(
                from_y.at[z, h], from_z.at[z, h], pzs.at[d, h], pzr.at[z, h], to_y
            ).wait_send()
        for step in (0, 2, 3):
            part_core(step, h).wait_send()
            part_y(step, h).wait_send()


def in_one_kernel(tokens, expert_ids, route_weights, gate_weight, up_weight, down_weight):
    rows, width = tokens.shape
    line = lax.axis_size("expert") // 2
    held, each, _ = gate_weight.shape
    units = held * each
    bf16 = jnp.bfloat16
    dma = pltpu.SemaphoreType.DMA
    vmem = pl.BlockSpec(memory_space=pltpu.VMEM)
    hbm = pl.BlockSpec(memory_space=pl.ANY)
    flat = (units, width)
    group_rows = line * 4 * rows
    return pl.pallas_call(
        functools.partial(kernel, line, held),
        out_shape=jax.ShapeDtypeStruct((rows, width), bf16),
        in_specs=[hbm, vmem, vmem, hbm, hbm, hbm],
        out_specs=vmem,
        scratch_shapes=[
            pltpu.VMEM((line, 2, 2, rows, width + EXTRA), bf16),
            pltpu.VMEM(flat, bf16),
            pltpu.VMEM(flat, bf16),
            pltpu.VMEM(flat, bf16),
            pltpu.VMEM((4 * rows, units), bf16),
            pltpu.VMEM((3, PIECES, 2, 2, rows, width // PIECES), bf16),
            pltpu.VMEM((line, PIECES, 2, rows, width // PIECES), bf16),
            pltpu.VMEM((line, PIECES, rows, width // PIECES), bf16),
            pltpu.VMEM((line + 1, PIECES, rows, width // PIECES), bf16),
            dma((3,)),
            dma,
            dma((line, 2)),
            dma((line,)),
            dma((line,)),
            dma((line,)),
            dma((line, 2)),
            dma((line, 2)),
            dma((line, PIECES)),
            dma((line, PIECES)),
            dma((line, PIECES)),
            dma((line, PIECES)),
            dma((line, PIECES)),
            dma((line + 1, PIECES)),
        ],
        compiler_params=pltpu.CompilerParams(
            collective_id=0, has_side_effects=True, vmem_limit_bytes=63 * 1024 * 1024
        ),
        cost_estimate=pl.CostEstimate(
            flops=6 * group_rows * units * width,
            bytes_accessed=6 * units * width,
            transcendentals=group_rows * units,
        ),
        name="experts",
    )(
        tokens, expert_ids, route_weights,
        gate_weight.reshape(flat), up_weight.reshape(flat), down_weight.reshape(flat),
    )


def in_steps(tokens, expert_ids, route_weights, gate_weight, up_weight, down_weight):
    held = gate_weight.shape[0]
    experts = held * lax.axis_size("expert")
    labels = jnp.arange(experts, dtype=jnp.int32)
    named = expert_ids[:, :, None] == labels[None, None, :]
    weights = jnp.sum(jnp.where(named, route_weights[:, :, None], 0.0), axis=1)
    group = ("expert", "tensor")
    rows = lax.all_gather(tokens, group, axis=0, tiled=True)
    all_weights = lax.all_gather(weights, group, axis=0, tiled=True)
    first = lax.axis_index("expert") * held
    mine = lax.dynamic_slice_in_dim(all_weights, first, held, axis=1)
    total, hidden_units = rows.shape[0], gate_weight.shape[1]
    flat = (held * hidden_units, gate_weight.shape[2])
    transposed = (((1,), (1,)), ((), ()))
    gate = lax.dot_general(
        rows, gate_weight.reshape(flat), transposed, preferred_element_type=jnp.float32
    )
    up = lax.dot_general(
        rows, up_weight.reshape(flat), transposed, preferred_element_type=jnp.float32
    )
    scaled = (jax.nn.silu(gate) * up).reshape(total, held, hidden_units) * mine[:, :, None]
    hidden = scaled.reshape(total, held * hidden_units).astype(jnp.bfloat16)
    partial = jnp.dot(hidden, down_weight.reshape(flat), preferred_element_type=jnp.float32)
    return lax.psum_scatter(
        partial.astype(jnp.bfloat16), group, scatter_dimension=0, tiled=True
    )


def solution(mesh):
    spread = P(("groups", "expert", "tensor"), None)
    weight = P("expert", "tensor", None)
    small = mesh.shape["expert"] == 8 and mesh.shape["tensor"] == 2
    return jax.shard_map(
        in_one_kernel if small else in_steps,
        mesh=mesh,
        in_specs=(spread,) * 3 + (weight,) * 3,
        out_specs=spread,
        check_vma=False,
    )
```
